256 devices in a mesh: inp: 32 (over z_hi, x, core), out: 8 (over z_lo, y).
Axes of the slice: x: 4, y: 4, z: 8 (z_hi: 4, z_lo: 2; z = z_hi * 2 + z_lo), core: 2. Of those that a mesh axis runs over, the one named last changes fastest.
Arguments:
- saved_inputs: bfloat16 [2, 1536, 8192], P(None, 'out', 'inp'), may hold values from -6 to 6
- output_grads: bfloat16 [2, 1536, 28672], P(None, 'inp', 'out'), may hold values from -0.15625 to 0.15625
- fisher_prior: float32 [8192, 28672], P('inp', 'out'), may hold values from 0.1 to 2
Outputs:
- fisher: float32 [8192, 28672], P('inp', 'out')
The draws below stay inside these ranges and needn't reach their ends.
All inputs are finite; a program needn't handle non-finite values.
Results may differ from the reference program's by a relative error of at most 0.0003.
Values may be sent and summed in bfloat16 or wider, within the bound.
No kernel may reach another device: no remote copies, remote signals or barrier semaphores. Data moves between devices by JAX's collectives and lax.ppermute only.
A program may use at most 128 MiB of HBM per device.

```python
import math
import jax
import jax.numpy as jnp

D = 8192
F = 28672
SEQ_LEN = 1536
SEQS = 2


def shard_levels(rng, extent, shards, smallest, top_value):
    def one(axis_at, blocks):
        steps = jax.random.uniform(jax.random.fold_in(jax.random.fold_in(rng, 6), axis_at), (blocks,), jnp.float32, smallest / len(shards), top_value / len(shards))
        return jnp.repeat(jnp.exp(steps), extent[axis_at] // blocks).reshape((-1,) + (1,) * (len(extent) - axis_at - 1))

    loudness = one(*shards[0])
    for cut in shards[1:]:
        loudness = loudness * one(*cut)
    return loudness


def centred(own_key, shape, deviation, most, pieces=(), dtype=jnp.bfloat16):
    array = deviation * jax.random.normal(own_key, shape, jnp.float32)
    if pieces:
        array = array * shard_levels(own_key, shape, pieces, -0.22, 0.18)
    return jnp.clip(array, -most, most).astype(dtype)


def setup_inputs(seed: int = 0) -> dict:
    seeds = jax.random.split(jax.random.key(seed), 4)
    return {
        "saved_inputs": centred(seeds[0], (SEQS, SEQ_LEN, D), 1.0, 6.0, ((1, 8), (2, 32))),
        "output_grads": centred(seeds[1], (SEQS, SEQ_LEN, F), SEQ_LEN ** -0.5, 0.15625, ((1, 32), (2, 8))),
        "fisher_prior": jnp.clip(jnp.exp(math.log(2.0) - 2.9957323 * jax.random.uniform(seeds[2], (D, F), jnp.float32) ** shard_levels(seeds[2], (D, F), ((0, 32), (1, 8)), -0.2, 0.2)), 0.1, 2.0),
    }


def reference(saved_inputs, output_grads, fisher_prior):
    squares = jnp.zeros((D, F), jnp.float32)
    for seq_index in range(SEQS):
        grad = jnp.dot(saved_inputs[seq_index].T, output_grads[seq_index], preferred_element_type=jnp.float32)
        squares = squares + grad * grad
    return 0.5 * fisher_prior + (0.5 / SEQS) * squares
```

```python
import functools

import jax
import jax.numpy as jnp
from jax import lax
from jax.experimental import pallas as pl
from jax.experimental.pallas import tpu as pltpu
from jax.sharding import PartitionSpec as P

ZH, XN, CN, ZL, YN = 4, 4, 2, 2, 4
AXES = ("inp", "out")
TILE = 256


def routes(dz=0, dx=0, dc=0):
    pairs = []
    for zh in range(ZH):
        for x in range(XN):
            for c in range(CN):
                here = (zh * XN + x) * CN + c
                there = ((zh + dz) % ZH * XN + (x + dx) % XN) * CN + (c + dc) % CN
                for out in range(ZL * YN):
                    pairs.append((there * ZL * YN + out, here * ZL * YN + out))
    return pairs


def fetch(v, **offset):
    return lax.ppermute(v, AXES, routes(**offset))


def gather_x(v):
    behind = fetch(v, dx=-1)
    ahead = fetch(v, dx=1)
    far0 = fetch(behind[0], dx=-1)
    far1 = fetch(ahead[1], dx=1)
    return [v, ahead, (far0, far1), behind]


def gather_z(v):
    behind = fetch(v, dz=-1)
    ahead = fetch(v, dz=1)
    far0 = fetch(behind[0], dz=-1)
    far1 = fetch(ahead[1], dz=1)
    return [v, ahead, jnp.stack([far0, far1]), behind]


def squares_kernel(layout, x_ref, *refs):
    out_ref = refs[-1]
    total = None
    for s in range(2):
        parts = []
        for first, whole in layout:
            if whole:
                parts.append(refs[first][s])
            else:
                parts.append(refs[first + s][...])
        rhs = jnp.concatenate(parts, axis=0)
        acc = jnp.dot(x_ref[s], rhs, preferred_element_type=jnp.float32)
        total = acc * acc if total is None else total + acc * acc
    out_ref[...] = total


def squares_of(xt, pieces):
    operands, specs, layout = [], [], []
    for p in pieces:
        if isinstance(p, tuple):
            layout.append((len(operands), False))
            for q in p:
                operands.append(q)
                specs.append(pl.BlockSpec((q.shape[0], TILE), lambda j: (0, j)))
        else:
            layout.append((len(operands), True))
            operands.append(p)
            specs.append(pl.BlockSpec((2, p.shape[1], TILE), lambda j: (0, 0, j)))
    w = operands[0].shape[-1]
    rows = xt.shape[1]
    return pl.pallas_call(
        functools.partial(squares_kernel, layout),
        grid=(w // TILE,),
        in_specs=[pl.BlockSpec(xt.shape, lambda j: (0, 0, 0))] + specs,
        out_specs=pl.BlockSpec((rows, TILE), lambda j: (0, j)),
        out_shape=jax.ShapeDtypeStruct((rows, w), jnp.float32),
        compiler_params=pltpu.CompilerParams(vmem_limit_bytes=32 * 2**20),
        cost_estimate=pl.CostEstimate(
            flops=4 * rows * xt.shape[2] * w,
            bytes_accessed=xt.size * 2 + 4 * xt.shape[2] * w + 4 * rows * w,
            transcendentals=0,
        ),
    )(xt, *operands)


def roll(v, axis, start):
    n = v.shape[axis]
    return lax.dynamic_slice_in_dim(jnp.concatenate([v, v], axis), start, n, axis)


def on_device(saved_inputs, output_grads, fisher_prior):
    inp = lax.axis_index("inp")
    core = inp % CN
    first = core == 0
    x = inp // CN % XN
    zh = inp // (CN * XN)
    seqs, toks, cols = output_grads.shape
    half = cols // 2
    narrow = TILE
    wide = half - narrow

    left, right = output_grads[..., :half], output_grads[..., half:]
    mine = jnp.where(first, left, right)
    got = fetch(jnp.where(first, right, left), dc=1)
    unit = jnp.concatenate([jnp.where(first, mine, got), jnp.where(first, got, mine)], axis=1)

    a = unit[..., :wide]
    b = unit[..., wide:]
    bx = gather_x(b)
    bx = jnp.concatenate([jnp.stack(p) if isinstance(p, tuple) else p for p in bx], axis=1)
    az = gather_z(a)
    pieces_a = []
    for p in az:
        pieces_a += gather_x(p)
    pieces_b = gather_z(bx)

    xs = lax.all_gather(saved_inputs, "out", axis=1, tiled=True)
    sib = fetch(xs, dc=1)
    xs = jnp.concatenate([jnp.where(first, xs, sib), jnp.where(first, sib, xs)], axis=2)
    feats = xs.shape[2]
    xs = xs.reshape(seqs, ZH, XN, CN * toks, feats)
    xs = roll(roll(xs, 1, zh), 2, x)
    xt = xs.reshape(seqs, ZH * XN * CN * toks, feats).swapaxes(1, 2)

    sq = jnp.concatenate([squares_of(xt, pieces_a), squares_of(xt, pieces_b)], axis=1)
    rows = feats // 2
    top, low = sq[:rows], sq[rows:]
    keep = jnp.where(first, top, low)
    back = fetch(jnp.where(first, low, top), dc=1)
    squares = jnp.concatenate([jnp.where(first, keep, back), jnp.where(first, back, keep)], axis=1)
    return 0.5 * fisher_prior + 0.5 / seqs * squares


def solution(mesh):
    in_specs = (P(None, "out", "inp"), P(None, "inp", "out"), P("inp", "out"))
    out_specs = P("inp", "out")
    return jax.shard_map(
        on_device, mesh=mesh, in_specs=in_specs, out_specs=out_specs, check_vma=False
    )
```

```python
import functools

import jax
import jax.numpy as jnp
from jax import lax
from jax.experimental import pallas as pl
from jax.experimental.pallas import tpu as pltpu
from jax.sharding import Mesh, PartitionSpec as P

SIZES = {"zh": 4, "x": 4, "c": 2, "zl": 2, "y": 4}
AXES = tuple(SIZES)
TILE = 256


def routes(offset):
    pairs = []
    for here in range(256):
        rest, there, scale = here, 0, 1
        for name in reversed(AXES):
            at, rest = rest % SIZES[name], rest // SIZES[name]
            there += (at + offset.get(name, 0)) % SIZES[name] * scale
            scale *= SIZES[name]
        pairs.append((there, here))
    return pairs


def fetch(v, **offset):
    return lax.ppermute(v, AXES, routes(offset))


def nothing(*refs):
    pass


def tie(values, after):
    n = len(values)
    anywhere = pl.BlockSpec(memory_space=pl.ANY)
    return pl.pallas_call(
        nothing,
        in_specs=[anywhere] * (n + len(after)),
        out_specs=[anywhere] * n,
        out_shape=[jax.ShapeDtypeStruct(v.shape, v.dtype) for v in values],
        input_output_aliases={i: i for i in range(n)},
        compiler_params=pltpu.CompilerParams(vmem_limit_bytes=2**20),
        cost_estimate=pl.CostEstimate(flops=0, bytes_accessed=0, transcendentals=0),
    )(*values, *after)


def stage(token, values, after=()):
    *values, token = tie((*values, token), after)
    (token,) = tie((token,), ())
    return values, token


def turn_kernel(at_ref, own_ref, own_far_ref, sib_ref, sib_far_ref, out_ref):
    zh, x, zl, y = at_ref[0], at_ref[1], at_ref[2], at_ref[3]
    rows = own_ref.shape[-1]
    group = own_ref.shape[2] // 2
    for dz in range(4):
        z_from = (zh + dz) % 4
        near = z_from // 2 == zl
        places = []
        for dx in range(4):
            x_from = (x + dx) % 4
            turn = (z_from % 2 * 2 + x_from // 2 + 4 - y) % 4
            places.append((turn, pl.ds(pl.multiple_of(x_from % 2 * group, 32), group)))

        def write(refs):
            for s in range(2):
                for k, ref in enumerate(refs):
                    block = jnp.concatenate([ref[turn, s, some] for turn, some in places], axis=0)
                    out_ref[s, k * rows : (k + 1) * rows, dz * 4 * group : (dz + 1) * 4 * group] = block.T

        pl.when(near)(functools.partial(write, (sib_ref, own_ref)))
        pl.when(jnp.logical_not(near))(functools.partial(write, (sib_far_ref, own_far_ref)))


VMEM = pl.BlockSpec(memory_space=pltpu.VMEM)


def turned(at, own, own_far, sib, sib_far):
    turns, seqs, toks, feats = own.shape
    return pl.pallas_call(
        turn_kernel,
        in_specs=[pl.BlockSpec(memory_space=pltpu.SMEM)] + [VMEM] * 4,
        out_specs=VMEM,
        out_shape=jax.ShapeDtypeStruct((seqs, 2 * feats, 2 * turns * toks), own.dtype),
        compiler_params=pltpu.CompilerParams(vmem_limit_bytes=16 * 2**20),
        cost_estimate=pl.CostEstimate(flops=0, bytes_accessed=16 * own.size, transcendentals=0),
    )(at, own, own_far, sib, sib_far)


def squares_kernel(layout, x_ref, *refs):
    *refs, theirs_ref, mine_ref = refs
    rows, w = theirs_ref.shape
    for tile in range(0, w, TILE):
        some = pl.ds(tile, TILE)
        total = None
        for s in range(2):
            rhs = jnp.concatenate([refs[p[s][0]][p[s][1] + (slice(None), some)] for p in layout], axis=0)
            acc = jnp.dot(x_ref[s], rhs, preferred_element_type=jnp.float32)
            total = acc * acc if total is None else total + acc * acc
        theirs_ref[:, some] = total[:rows]
        mine_ref[:, some] = total[rows:]


def squares_of(xt, pieces):
    operands, layout = [], []
    for piece in pieces:
        views = []
        for array, index in piece:
            k = next((k for k, o in enumerate(operands) if o is array), None)
            if k is None:
                k = len(operands)
                operands.append(array)
            views.append((k, index))
        layout.append(views)
    rows, w = xt.shape[1] // 2, operands[0].shape[-1]
    return pl.pallas_call(
        functools.partial(squares_kernel, layout),
        in_specs=[VMEM] * (1 + len(operands)),
        out_specs=[VMEM] * 2,
        out_shape=[jax.ShapeDtypeStruct((rows, w), jnp.float32)] * 2,
        compiler_params=pltpu.CompilerParams(vmem_limit_bytes=16 * 2**20),
        cost_estimate=pl.CostEstimate(
            flops=8 * rows * xt.shape[2] * w,
            bytes_accessed=xt.size * 2 + 4 * xt.shape[2] * w + 8 * rows * w,
            transcendentals=0,
        ),
    )(xt, *operands)


def both(array, *index):
    return [(array, index + (0,)), (array, index + (1,))]


def in_order(first, mine, other, axis):
    return jnp.concatenate([jnp.where(first, mine, other), jnp.where(first, other, mine)], axis)


def on_device(saved_inputs, output_grads, fisher_prior):
    first = lax.axis_index("c") == 0
    at = jnp.stack([lax.axis_index(name) for name in ("zh", "x", "zl", "y")]).astype(jnp.int32)
    seqs, toks, cols = output_grads.shape
    half = cols // 2
    token = jnp.zeros((8, 128), jnp.float32)

    left, right = output_grads[..., :half], output_grads[..., half:]
    got = fetch(jnp.where(first, right, left), c=1)
    unit = in_order(first, jnp.where(first, left, right), got, 1)

    (unit,), token = stage(token, (unit,))
    above0, below0 = fetch(unit[0], zh=1), fetch(unit[0], zh=-1)
    ahead, behind = fetch(unit, x=1), fetch(unit, x=-1)
    turn1 = fetch(saved_inputs, y=1)

    (above0, below0, ahead, behind, turn1), token = stage(token, (above0, below0, ahead, behind, turn1))
    above1, below1 = fetch(unit[1], zh=1), fetch(unit[1], zh=-1)
    first_ahead = fetch(jnp.stack([ahead[1], above0, below0]), x=1)
    first_behind = fetch(jnp.stack([behind[0], above0, below0]), x=-1)
    turn2 = fetch(turn1, y=1)

    (above1, below1, turn2), token = stage(token, (above1, below1, turn2))
    sides = jnp.stack([above1, below1])
    second_ahead, second_behind = fetch(sides, x=1), fetch(sides, x=-1)
    turn3 = fetch(turn2, y=1)

    (first_ahead, first_behind, below0, above1, turn3), token = stage(token, (first_ahead, first_behind, below0, above1, turn3))
    opp0, opp1 = fetch(below0, zh=-1), fetch(above1, zh=1)
    turns = jnp.stack([saved_inputs, turn1, turn2, turn3])

    (second_ahead, second_behind), token = stage(token, (second_ahead, second_behind))
    above_far = fetch(jnp.stack([first_behind[1], second_behind[0]]), x=-1)
    below_far = fetch(jnp.stack([first_ahead[2], second_ahead[1]]), x=1)

    (opp0, opp1, turns), token = stage(token, (opp0, opp1, turns))
    opp = jnp.stack([opp0, opp1])
    opp_ahead, opp_behind = fetch(opp, x=1), fetch(opp, x=-1)
    met = fetch(turns, zl=1)

    (opp_ahead, opp_behind, met), token = stage(token, (opp_ahead, opp_behind, met))
    opp_far0, opp_far1 = fetch(opp_behind[0], x=-1), fetch(opp_ahead[1], x=1)
    sib, sib_met = fetch(turns, c=1), fetch(met, c=1)
    xt = turned(at, turns, met, sib, sib_met)

    pieces = [both(unit), both(ahead), [(first_behind, (0,)), (first_ahead, (0,))], both(behind)]
    pieces.append([(above0, ()), (above1, ())])
    pieces.append([(first_ahead, (1,)), (second_ahead, (0,))])
    pieces.append(both(above_far))
    pieces.append([(first_behind, (1,)), (second_behind, (0,))])
    pieces += [both(opp), both(opp_ahead), [(opp_far0, ()), (opp_far1, ())], both(opp_behind)]
    pieces.append([(below0, ()), (below1, ())])
    pieces.append([(first_ahead, (2,)), (second_ahead, (1,))])
    pieces.append(both(below_far))
    pieces.append([(first_behind, (2,)), (second_behind, (1,))])
    theirs, mine = squares_of(xt, pieces)
    squares = in_order(first, mine, fetch(theirs, c=1), 1)
    return 0.5 * fisher_prior + 0.5 / seqs * squares


def solution(mesh):
    fine = Mesh(mesh.devices.reshape(tuple(SIZES.values())), AXES)
    inp, out = ("zh", "x", "c"), ("zl", "y")
    return jax.shard_map(
        on_device,
        mesh=fine,
        in_specs=(P(None, out, inp), P(None, inp, out), P(inp, out)),
        out_specs=P(inp, out),
        check_vma=False,
    )
```

```python
import functools

import jax
import jax.numpy as jnp
from jax import lax
from jax.experimental import pallas as pl
from jax.experimental.pallas import tpu as pltpu
from jax.sharding import Mesh, PartitionSpec as P

SIZES = {"zh": 4, "x": 4, "c": 2, "zl": 2, "y": 4}
AXES = tuple(SIZES)
TILE = 256


def routes(offset):
    pairs = []
    for here in range(256):
        rest, there, scale = here, 0, 1
        for name in reversed(AXES):
            at, rest = rest % SIZES[name], rest // SIZES[name]
            there += (at + offset.get(name, 0)) % SIZES[name] * scale
            scale *= SIZES[name]
        pairs.append((there, here))
    return pairs


def fetch(v, **offset):
    return lax.ppermute(v, AXES, routes(offset))


def nothing(*refs):
    pass


def tie(values, after):
    n = len(values)
    anywhere = pl.BlockSpec(memory_space=pl.ANY)
    return pl.pallas_call(
        nothing,
        in_specs=[anywhere] * (n + len(after)),
        out_specs=[anywhere] * n,
        out_shape=[jax.ShapeDtypeStruct(v.shape, v.dtype) for v in values],
        input_output_aliases={i: i for i in range(n)},
        compiler_params=pltpu.CompilerParams(vmem_limit_bytes=2**20),
        cost_estimate=pl.CostEstimate(flops=0, bytes_accessed=0, transcendentals=0),
    )(*values, *after)


def stage(token, values, after=()):
    *values, token = tie((*values, token), after)
    (token,) = tie((token,), ())
    return values, token


def turn_kernel(at_ref, own_ref, own_far_ref, sib_ref, sib_far_ref, out_ref, all_ref):
    zh, x, zl, y = at_ref[0], at_ref[1], at_ref[2], at_ref[3]
    rows = own_ref.shape[-1]
    group = own_ref.shape[2] // 2
    for far, refs in enumerate(((sib_ref, own_ref), (sib_far_ref, own_far_ref))):
        for k, ref in enumerate(refs):
            all_ref[far, :, :, :, k * rows : (k + 1) * rows] = ref[...]
    for four in range(4):
        places = []
        for dz, dx in ORDER[4 * four : 4 * four + 4]:
            z_from, x_from = (zh + dz) % 4, (x + dx) % 4
            far = (z_from // 2 + zl) % 2
            turn = (z_from % 2 * 2 + x_from // 2 + 4 - y) % 4
            places.append((far, turn, pl.ds(pl.multiple_of(x_from % 2 * group, 32), group)))
        for s in range(2):
            block = jnp.concatenate([all_ref[far, turn, s, some] for far, turn, some in places], axis=0)
            out_ref[s, :, four * 4 * group : (four + 1) * 4 * group] = block.T


VMEM = pl.BlockSpec(memory_space=pltpu.VMEM)
ORDER = ((0, 0), (0, 1), (0, 2), (0, 3), (1, 0), (1, 1), (1, 3), (3, 0), (3, 1), (3, 3), (2, 0), (2, 1))
ORDER += ((2, 3), (1, 2), (2, 2), (3, 2))


def turned(at, own, own_far, sib, sib_far):
    turns, seqs, toks, feats = own.shape
    return pl.pallas_call(
        turn_kernel,
        in_specs=[pl.BlockSpec(memory_space=pltpu.SMEM)] + [VMEM] * 4,
        out_specs=VMEM,
        out_shape=jax.ShapeDtypeStruct((seqs, 2 * feats, 2 * turns * toks), own.dtype),
        scratch_shapes=[pltpu.VMEM((2, turns, seqs, toks, 2 * feats), own.dtype)],
        compiler_params=pltpu.CompilerParams(vmem_limit_bytes=8 * 2**20),
        cost_estimate=pl.CostEstimate(flops=0, bytes_accessed=16 * own.size, transcendentals=0),
    )(at, own, own_far, sib, sib_far)


def listed(runs):
    operands, spans = [], []
    for start, pieces in runs:
        layout = []
        for piece in pieces:
            views = []
            for array, index in piece:
                k = next((k for k, o in enumerate(operands) if o is array), None)
                if k is None:
                    k = len(operands)
                    operands.append(array)
                views.append((k, index))
            layout.append(views)
        spans.append((start, layout))
    return operands, spans


def products(spans, x_ref, refs, s, some):
    total = None
    for start, layout in spans:
        rhs = jnp.concatenate([refs[p[s][0]][p[s][1] + (slice(None), some)] for p in layout], axis=0)
        part = jnp.dot(x_ref[s, :, start : start + rhs.shape[0]], rhs, preferred_element_type=jnp.float32)
        total = part if total is None else total + part
    return total


def early_kernel(spans, prior_ref, x_ref, *refs):
    *refs, sums_ref, base_ref = refs
    w = sums_ref.shape[2]
    for tile in range(0, w, TILE):
        some = pl.ds(tile, TILE)
        for s in range(2):
            sums_ref[s, :, some] = products(spans, x_ref, refs, s, some)
        for side in (some, pl.ds(w + tile, TILE)):
            base_ref[:, side] = 0.5 * prior_ref[:, side]


def late_kernel(spans, at_ref, sums_ref, base_ref, x_ref, *refs):
    *refs, theirs_ref, out_ref = refs
    rows, w = theirs_ref.shape
    for tile in range(0, w, TILE):
        some = pl.ds(tile, TILE)
        total = None
        for s in range(2):
            acc = sums_ref[s, :, some] + products(spans, x_ref, refs, s, some)
            total = acc * acc if total is None else total + acc * acc
        theirs_ref[:, some] = total[:rows]
        mine = pl.ds(pl.multiple_of(at_ref[4] * w + tile, TILE), TILE)
        other = pl.ds(pl.multiple_of((1 - at_ref[4]) * w + tile, TILE), TILE)
        out_ref[:, mine] = base_ref[:, mine] + 0.25 * total[rows:]
        out_ref[:, other] = base_ref[:, other]


def early_sums(prior, xt, runs):
    operands, spans = listed(runs)
    rows, cols = prior.shape
    return pl.pallas_call(
        functools.partial(early_kernel, spans),
        in_specs=[VMEM] * (2 + len(operands)),
        out_specs=[VMEM] * 2,
        out_shape=[
            jax.ShapeDtypeStruct((2, 2 * rows, cols // 2), jnp.float32),
            jax.ShapeDtypeStruct(prior.shape, jnp.float32),
        ],
        compiler_params=pltpu.CompilerParams(vmem_limit_bytes=8 * 2**20),
        cost_estimate=pl.CostEstimate(flops=3 * rows * xt.shape[2] * cols, bytes_accessed=0, transcendentals=0),
    )(prior, xt, *operands)


def late_squares(at, sums, base, xt, runs):
    operands, spans = listed(runs)
    rows, cols = base.shape
    return pl.pallas_call(
        functools.partial(late_kernel, spans),
        in_specs=[pl.BlockSpec(memory_space=pltpu.SMEM)] + [VMEM] * (3 + len(operands)),
        out_specs=[VMEM] * 2,
        out_shape=[
            jax.ShapeDtypeStruct((rows, cols // 2), jnp.float32),
            jax.ShapeDtypeStruct(base.shape, jnp.float32),
        ],
        compiler_params=pltpu.CompilerParams(vmem_limit_bytes=8 * 2**20),
        cost_estimate=pl.CostEstimate(flops=rows * xt.shape[2] * cols, bytes_accessed=0, transcendentals=0),
    )(at, sums, base, xt, *operands)


def both(array, *index):
    return [(array, index + (0,)), (array, index + (1,))]


def in_order(first, mine, other, axis):
    return jnp.concatenate([jnp.where(first, mine, other), jnp.where(first, other, mine)], axis)


def on_device(saved_inputs, output_grads, fisher_prior):
    first = lax.axis_index("c") == 0
    at = jnp.stack([lax.axis_index(name) for name in ("zh", "x", "zl", "y", "c")]).astype(jnp.int32)
    seqs, toks, cols = output_grads.shape
    half = cols // 2
    token = jnp.zeros((8, 128), jnp.float32)

    left, right = output_grads[..., :half], output_grads[..., half:]
    got = fetch(jnp.where(first, right, left), c=1)
    unit = in_order(first, jnp.where(first, left, right), got, 1)

    unit0, unit1 = unit[0], unit[1]
    (unit, unit0, unit1), token = stage(token, (unit, unit0, unit1))
    above0, below0 = fetch(unit0, zh=1), fetch(unit0, zh=-1)
    ahead, behind = fetch(unit, x=1), fetch(unit, x=-1)
    turn1 = fetch(saved_inputs, y=1)

    (above0, below0, ahead, behind, turn1, unit1), token = stage(token, (above0, below0, ahead, behind, turn1, unit1))
    above1, below1 = fetch(unit1, zh=1), fetch(unit1, zh=-1)
    first_ahead = fetch(jnp.stack([ahead[1], above0, below0]), x=1)
    first_behind = fetch(jnp.stack([behind[0], above0, below0]), x=-1)
    turn2 = fetch(turn1, y=1)

    (above1, below1, below0, turn2), token = stage(token, (above1, below1, below0, turn2))
    opp0, opp1 = fetch(below0, zh=-1), fetch(above1, zh=1)

    sides = jnp.stack([above1, below1])
    (sides, turn2), token = stage(token, (sides, turn2), (first_ahead, first_behind))
    second_ahead, second_behind = fetch(sides, x=1), fetch(sides, x=-1)
    turn3 = fetch(turn2, y=1)
    turns = jnp.stack([saved_inputs, turn1, turn2, turn3])

    (opp0, opp1, turns), token = stage(token, (opp0, opp1, turns))
    opp = jnp.stack([opp0, opp1])
    opp_ahead, opp_behind = fetch(opp, x=1), fetch(opp, x=-1)
    met = fetch(turns, zl=1)

    (second_ahead, second_behind), token = stage(token, (second_ahead, second_behind))
    above_far = fetch(jnp.stack([first_behind[1], second_behind[0]]), x=-1)
    below_far = fetch(jnp.stack([first_ahead[2], second_ahead[1]]), x=1)

    (opp_ahead, opp_behind), token = stage(token, (opp_ahead, opp_behind))
    opp_far0, opp_far1 = fetch(opp_behind[0], x=-1), fetch(opp_ahead[1], x=1)
    sib, sib_met = fetch(turns, c=1), fetch(met, c=1)
    xt = turned(at, turns, met, sib, sib_met)

    early = [both(unit), both(ahead), [(first_behind, (0,)), (first_ahead, (0,))], both(behind)]
    early.append([(above0, ()), (above1, ())])
    early.append([(first_ahead, (1,)), (second_ahead, (0,))])
    early.append([(first_behind, (1,)), (second_behind, (0,))])
    early.append([(below0, ()), (below1, ())])
    early.append([(first_ahead, (2,)), (second_ahead, (1,))])
    early.append([(first_behind, (2,)), (second_behind, (1,))])
    early += [both(opp), both(opp_ahead)]
    late = [both(opp_behind), both(above_far), [(opp_far0, ()), (opp_far1, ())], both(below_far)]
    sums, base = early_sums(fisher_prior, xt, [(0, early)])
    runs = [(len(early) * 2 * toks, late)]
    theirs, out = late_squares(at, sums, base, xt, runs)
    back = 0.25 * fetch(theirs, c=1)
    return out + in_order(first, jnp.zeros_like(back), back, 1)


def solution(mesh):
    fine = Mesh(mesh.devices.reshape(tuple(SIZES.values())), AXES)
    inp, out = ("zh", "x", "c"), ("zl", "y")
    return jax.shard_map(
        on_device,
        mesh=fine,
        in_specs=(P(None, out, inp), P(None, inp, out), P(inp, out)),
        out_specs=P(inp, out),
        check_vma=False,
    )
```

```python
import functools

import jax
import jax.numpy as jnp
from jax import lax
from jax.experimental import pallas as pl
from jax.experimental.pallas import tpu as pltpu
from jax.sharding import Mesh, PartitionSpec as P

SIZES = {"zh": 4, "x": 4, "c": 2, "zl": 2, "y": 4}
AXES = tuple(SIZES)
TILE = 256


def routes(offset):
    pairs = []
    for here in range(256):
        rest, there, scale = here, 0, 1
        for name in reversed(AXES):
            at, rest = rest % SIZES[name], rest // SIZES[name]
            there += (at + offset.get(name, 0)) % SIZES[name] * scale
            scale *= SIZES[name]
        pairs.append((there, here))
    return pairs


def fetch(v, **offset):
    return lax.ppermute(v, AXES, routes(offset))


def nothing(*refs):
    pass


def tie(values, after):
    n = len(values)
    anywhere = pl.BlockSpec(memory_space=pl.ANY)
    return pl.pallas_call(
        nothing,
        in_specs=[anywhere] * (n + len(after)),
        out_specs=[anywhere] * n,
        out_shape=[jax.ShapeDtypeStruct(v.shape, v.dtype) for v in values],
        input_output_aliases={i: i for i in range(n)},
        compiler_params=pltpu.CompilerParams(vmem_limit_bytes=2**20),
        cost_estimate=pl.CostEstimate(flops=0, bytes_accessed=0, transcendentals=0),
    )(*values, *after)


def stage(token, values, after=()):
    *values, token = tie((*values, token), after)
    (token,) = tie((token,), ())
    return values, token


def turn_kernel(at_ref, own_ref, own_far_ref, sib_ref, sib_far_ref, out_ref, all_ref):
    zh, x, zl, y = at_ref[0], at_ref[1], at_ref[2], at_ref[3]
    rows = own_ref.shape[-1]
    group = own_ref.shape[2] // 2
    for far, refs in enumerate(((sib_ref, own_ref), (sib_far_ref, own_far_ref))):
        for k, ref in enumerate(refs):
            all_ref[far, :, :, :, k * rows : (k + 1) * rows] = ref[...]
    for four in range(4):
        places = []
        for dz, dx in ORDER[4 * four : 4 * four + 4]:
            z_from, x_from = (zh + dz) % 4, (x + dx) % 4
            far = (z_from // 2 + zl) % 2
            turn = (z_from % 2 * 2 + x_from // 2 + 4 - y) % 4
            places.append((far, turn, pl.ds(pl.multiple_of(x_from % 2 * group, 32), group)))
        for s in range(2):
            block = jnp.concatenate([all_ref[far, turn, s, some] for far, turn, some in places], axis=0)
            out_ref[s, :, four * 4 * group : (four + 1) * 4 * group] = block.T


VMEM = pl.BlockSpec(memory_space=pltpu.VMEM)
ORDER = ((0, 0), (0, 1), (0, 2), (0, 3), (1, 0), (1, 1), (1, 3), (3, 0), (3, 1), (3, 3), (2, 0), (2, 1))
ORDER += ((2, 3), (1, 2), (2, 2), (3, 2))


def turned(at, own, own_far, sib, sib_far):
    turns, seqs, toks, feats = own.shape
    return pl.pallas_call(
        turn_kernel,
        in_specs=[pl.BlockSpec(memory_space=pltpu.SMEM)] + [VMEM] * 4,
        out_specs=VMEM,
        out_shape=jax.ShapeDtypeStruct((seqs, 2 * feats, 2 * turns * toks), own.dtype),
        scratch_shapes=[pltpu.VMEM((2, turns, seqs, toks, 2 * feats), own.dtype)],
        compiler_params=pltpu.CompilerParams(vmem_limit_bytes=8 * 2**20),
        cost_estimate=pl.CostEstimate(flops=0, bytes_accessed=16 * own.size, transcendentals=0),
    )(at, own, own_far, sib, sib_far)


def listed(runs):
    operands, spans = [], []
    for start, pieces in runs:
        layout = []
        for piece in pieces:
            views = []
            for array, index in piece:
                k = next((k for k, o in enumerate(operands) if o is array), None)
                if k is None:
                    k = len(operands)
                    operands.append(array)
                views.append((k, index))
            layout.append(views)
        spans.append((start, layout))
    return operands, spans


def products(spans, x_ref, refs, s, some, rows=slice(None)):
    total = None
    for start, layout in spans:
        rhs = jnp.concatenate([refs[p[s][0]][p[s][1] + (slice(None), some)] for p in layout], axis=0)
        part = jnp.dot(x_ref[s, rows, start : start + rhs.shape[0]], rhs, preferred_element_type=jnp.float32)
        total = part if total is None else total + part
    return total


def early_kernel(spans, prior_ref, x_ref, *refs):
    *refs, sums_ref, base_ref = refs
    w = sums_ref.shape[2]
    for tile in range(0, w, TILE):
        some = pl.ds(tile, TILE)
        for s in range(2):
            sums_ref[s, :, some] = products(spans, x_ref, refs, s, some)
        for side in (some, pl.ds(w + tile, TILE)):
            base_ref[:, side] = 0.5 * prior_ref[:, side]


def late_tile(spans, sums_ref, x_ref, refs, some, rows):
    total = None
    for s in range(2):
        acc = sums_ref[s, rows, some] + products(spans, x_ref, refs, s, some, rows)
        total = acc * acc if total is None else total + acc * acc
    return total


def theirs_kernel(spans, sums_ref, x_ref, *refs):
    *refs, out_ref = refs
    rows, w = out_ref.shape
    for tile in range(0, w, TILE):
        some = pl.ds(tile, TILE)
        out_ref[:, some] = late_tile(spans, sums_ref, x_ref, refs, some, pl.ds(0, rows))


def mine_kernel(spans, at_ref, base_ref, sums_ref, x_ref, *refs):
    *refs, out_ref = refs
    rows, w = out_ref.shape[0], sums_ref.shape[2]
    for tile in range(0, w, TILE):
        total = late_tile(spans, sums_ref, x_ref, refs, pl.ds(tile, TILE), pl.ds(rows, rows))
        mine = pl.ds(pl.multiple_of(at_ref[4] * w + tile, TILE), TILE)
        other = pl.ds(pl.multiple_of((1 - at_ref[4]) * w + tile, TILE), TILE)
        out_ref[:, mine] = base_ref[:, mine] + 0.25 * total
        out_ref[:, other] = base_ref[:, other]


def early_sums(prior, xt, runs):
    operands, spans = listed(runs)
    rows, cols = prior.shape
    return pl.pallas_call(
        functools.partial(early_kernel, spans),
        in_specs=[VMEM] * (2 + len(operands)),
        out_specs=[VMEM] * 2,
        out_shape=[
            jax.ShapeDtypeStruct((2, 2 * rows, cols // 2), jnp.float32),
            jax.ShapeDtypeStruct(prior.shape, jnp.float32),
        ],
        compiler_params=pltpu.CompilerParams(vmem_limit_bytes=8 * 2**20),
        cost_estimate=pl.CostEstimate(flops=3 * rows * xt.shape[2] * cols, bytes_accessed=0, transcendentals=0),
    )(prior, xt, *operands)


def late_call(kernel, first, specs, sums, xt, runs, shape):
    operands, spans = listed(runs)
    return pl.pallas_call(
        functools.partial(kernel, spans),
        in_specs=specs + [VMEM] * (2 + len(operands)),
        out_specs=VMEM,
        out_shape=jax.ShapeDtypeStruct(shape, jnp.float32),
        compiler_params=pltpu.CompilerParams(vmem_limit_bytes=8 * 2**20),
        cost_estimate=pl.CostEstimate(flops=sums.size * 500, bytes_accessed=0, transcendentals=0),
    )(*first, sums, xt, *operands)


def late_theirs(sums, xt, runs):
    return late_call(theirs_kernel, (), [], sums, xt, runs, (sums.shape[1] // 2, sums.shape[2]))


def late_mine(at, base, sums, xt, runs):
    return late_call(mine_kernel, (at, base), [pl.BlockSpec(memory_space=pltpu.SMEM), VMEM], sums, xt, runs, base.shape)


def both(array, *index):
    return [(array, index + (0,)), (array, index + (1,))]


def in_order(first, mine, other, axis):
    return jnp.concatenate([jnp.where(first, mine, other), jnp.where(first, other, mine)], axis)


def on_device(saved_inputs, output_grads, fisher_prior):
    first = lax.axis_index("c") == 0
    at = jnp.stack([lax.axis_index(name) for name in ("zh", "x", "zl", "y", "c")]).astype(jnp.int32)
    seqs, toks, cols = output_grads.shape
    half = cols // 2
    token = jnp.zeros((8, 128), jnp.float32)

    left, right = output_grads[..., :half], output_grads[..., half:]
    got = fetch(jnp.where(first, right, left), c=1)
    unit = in_order(first, jnp.where(first, left, right), got, 1)

    unit0, unit1 = unit[0], unit[1]
    (unit, unit0, unit1), token = stage(token, (unit, unit0, unit1))
    above0, below0 = fetch(unit0, zh=1), fetch(unit0, zh=-1)
    ahead, behind = fetch(unit, x=1), fetch(unit, x=-1)
    turn1 = fetch(saved_inputs, y=1)

    (above0, below0, ahead, behind, turn1, unit1), token = stage(token, (above0, below0, ahead, behind, turn1, unit1))
    above1, below1 = fetch(unit1, zh=1), fetch(unit1, zh=-1)
    first_ahead = fetch(jnp.stack([ahead[1], above0, below0]), x=1)
    first_behind = fetch(jnp.stack([behind[0], above0, below0]), x=-1)
    turn2 = fetch(turn1, y=1)

    (above1, below1, below0, turn2), token = stage(token, (above1, below1, below0, turn2))
    opp0, opp1 = fetch(below0, zh=-1), fetch(above1, zh=1)

    sides = jnp.stack([above1, below1])
    (sides, turn2), token = stage(token, (sides, turn2), (first_ahead, first_behind))
    second_ahead, second_behind = fetch(sides, x=1), fetch(sides, x=-1)
    turn3 = fetch(turn2, y=1)
    turns = jnp.stack([saved_inputs, turn1, turn2, turn3])

    (opp0, opp1, turns), token = stage(token, (opp0, opp1, turns))
    opp = jnp.stack([opp0, opp1])
    opp_ahead, opp_behind = fetch(opp, x=1), fetch(opp, x=-1)
    met = fetch(turns, zl=1)

    (second_ahead, second_behind), token = stage(token, (second_ahead, second_behind))
    above_far = fetch(jnp.stack([first_behind[1], second_behind[0]]), x=-1)
    below_far = fetch(jnp.stack([first_ahead[2], second_ahead[1]]), x=1)

    (opp_ahead, opp_behind, turns), token = stage(token, (opp_ahead, opp_behind, turns))
    opp_far0, opp_far1 = fetch(opp_behind[0], x=-1), fetch(opp_ahead[1], x=1)
    sib, sib_met = fetch(turns, c=1), fetch(met, c=1)
    xt = turned(at, turns, met, sib, sib_met)

    early = [both(unit), both(ahead), [(first_behind, (0,)), (first_ahead, (0,))], both(behind)]
    early.append([(above0, ()), (above1, ())])
    early.append([(first_ahead, (1,)), (second_ahead, (0,))])
    early.append([(first_behind, (1,)), (second_behind, (0,))])
    early.append([(below0, ()), (below1, ())])
    early.append([(first_ahead, (2,)), (second_ahead, (1,))])
    early.append([(first_behind, (2,)), (second_behind, (1,))])
    early += [both(opp), both(opp_ahead)]
    late = [both(opp_behind), both(above_far), [(opp_far0, ()), (opp_far1, ())], both(below_far)]
    sums, base = early_sums(fisher_prior, xt, [(0, early)])
    runs = [(len(early) * 2 * toks, late)]
    back = 0.25 * fetch(late_theirs(sums, xt, runs), c=1)
    out = late_mine(at, base, sums, xt, runs)
    return out + in_order(first, jnp.zeros_like(back), back, 1)


def solution(mesh):
    fine = Mesh(mesh.devices.reshape(tuple(SIZES.values())), AXES)
    inp, out = ("zh", "x", "c"), ("zl", "y")
    return jax.shard_map(
        on_device,
        mesh=fine,
        in_specs=(P(None, out, inp), P(None, inp, out), P(inp, out)),
        out_specs=P(inp, out),
        check_vma=False,
    )
```

```python
import functools

import jax
import jax.numpy as jnp
from jax import lax
from jax.experimental import pallas as pl
from jax.experimental.pallas import tpu as pltpu
from jax.sharding import Mesh, PartitionSpec as P

SIZES = {"zh": 4, "x": 4, "c": 2, "zl": 2, "y": 4}
AXES = tuple(SIZES)
TILE = 256


def routes(offset):
    pairs = []
    for here in range(256):
        rest, there, scale = here, 0, 1
        for name in reversed(AXES):
            at, rest = rest % SIZES[name], rest // SIZES[name]
            there += (at + offset.get(name, 0)) % SIZES[name] * scale
            scale *= SIZES[name]
        pairs.append((there, here))
    return pairs


def fetch(v, **offset):
    return lax.ppermute(v, AXES, routes(offset))


def nothing(*refs):
    pass


def tie(values, after):
    n = len(values)
    anywhere = pl.BlockSpec(memory_space=pl.ANY)
    return pl.pallas_call(
        nothing,
        in_specs=[anywhere] * (n + len(after)),
        out_specs=[anywhere] * n,
        out_shape=[jax.ShapeDtypeStruct(v.shape, v.dtype) for v in values],
        input_output_aliases={i: i for i in range(n)},
        compiler_params=pltpu.CompilerParams(vmem_limit_bytes=2**20),
        cost_estimate=pl.CostEstimate(flops=0, bytes_accessed=0, transcendentals=0),
    )(*values, *after)


def stage(token, values, after=()):
    *values, token = tie((*values, token), after)
    (token,) = tie((token,), ())
    return values, token


def turn_kernel(at_ref, own_ref, own_far_ref, sib_ref, sib_far_ref, out_ref, all_ref):
    zh, x, zl, y = at_ref[0], at_ref[1], at_ref[2], at_ref[3]
    rows = own_ref.shape[-1]
    group = own_ref.shape[2] // 2
    for far, refs in enumerate(((sib_ref, own_ref), (sib_far_ref, own_far_ref))):
        for k, ref in enumerate(refs):
            all_ref[far, :, :, :, k * rows : (k + 1) * rows] = ref[...]
    for four in range(4):
        places = []
        for dz, dx in ORDER[4 * four : 4 * four + 4]:
            z_from, x_from = (zh + dz) % 4, (x + dx) % 4
            far = (z_from // 2 + zl) % 2
            turn = (z_from % 2 * 2 + x_from // 2 + 4 - y) % 4
            for core in (at_ref[4], 1 - at_ref[4]):
                start = x_from % 2 * group + core * (group // 2)
                places.append((far, turn, pl.ds(pl.multiple_of(start, 16), group // 2)))
        for s in range(2):
            block = jnp.concatenate([all_ref[far, turn, s, some] for far, turn, some in places], axis=0)
            out_ref[s, :, four * 4 * group : (four + 1) * 4 * group] = block.T


VMEM = pl.BlockSpec(memory_space=pltpu.VMEM)
ORDER = ((0, 0), (0, 1), (0, 2), (0, 3), (1, 0), (1, 1), (1, 3), (3, 0), (3, 1), (3, 3), (2, 0), (2, 1))
ORDER += ((2, 3), (1, 2), (2, 2), (3, 2))


def turned(at, own, own_far, sib, sib_far):
    turns, seqs, toks, feats = own.shape
    return pl.pallas_call(
        turn_kernel,
        in_specs=[pl.BlockSpec(memory_space=pltpu.SMEM)] + [VMEM] * 4,
        out_specs=VMEM,
        out_shape=jax.ShapeDtypeStruct((seqs, 2 * feats, 2 * turns * toks), own.dtype),
        scratch_shapes=[pltpu.VMEM((2, turns, seqs, toks, 2 * feats), own.dtype)],
        compiler_params=pltpu.CompilerParams(vmem_limit_bytes=8 * 2**20),
        cost_estimate=pl.CostEstimate(flops=0, bytes_accessed=16 * own.size, transcendentals=0),
    )(at, own, own_far, sib, sib_far)


def listed(runs):
    operands, spans = [], []
    for start, pieces in runs:
        layout = []
        for piece in pieces:
            views = []
            for array, index in piece:
                k = next((k for k, o in enumerate(operands) if o is array), None)
                if k is None:
                    k = len(operands)
                    operands.append(array)
                views.append((k, index))
            layout.append(views)
        spans.append((start, layout))
    return operands, spans


def products(spans, x_ref, refs, s, some, rows=slice(None)):
    total = None
    for start, layout in spans:
        rhs = jnp.concatenate([refs[p[s][0]][p[s][1] + (slice(None), some)] for p in layout], axis=0)
        part = jnp.dot(x_ref[s, rows, start : start + rhs.shape[0]], rhs, preferred_element_type=jnp.float32)
        total = part if total is None else total + part
    return total


def early_kernel(spans, prior_ref, x_ref, *refs):
    *refs, sums_ref, base_ref = refs
    w = sums_ref.shape[2]
    for tile in range(0, w, TILE):
        some = pl.ds(tile, TILE)
        for s in range(2):
            sums_ref[s, :, some] = products(spans, x_ref, refs, s, some)
        for side in (some, pl.ds(w + tile, TILE)):
            base_ref[:, side] = 0.5 * prior_ref[:, side]


def late_tile(spans, sums_ref, x_ref, refs, some, rows):
    total = None
    for s in range(2):
        acc = sums_ref[s, rows, some] + products(spans, x_ref, refs, s, some, rows)
        total = acc * acc if total is None else total + acc * acc
    return total


def theirs_kernel(spans, sums_ref, x_ref, *refs):
    *refs, out_ref = refs
    rows, w = out_ref.shape
    for tile in range(0, w, TILE):
        some = pl.ds(tile, TILE)
        out_ref[:, some] = late_tile(spans, sums_ref, x_ref, refs, some, pl.ds(0, rows))


def mine_kernel(spans, at_ref, base_ref, sums_ref, x_ref, *refs):
    *refs, out_ref = refs
    rows, w = out_ref.shape[0], sums_ref.shape[2]
    for tile in range(0, w, TILE):
        total = late_tile(spans, sums_ref, x_ref, refs, pl.ds(tile, TILE), pl.ds(rows, rows))
        mine = pl.ds(pl.multiple_of(at_ref[4] * w + tile, TILE), TILE)
        other = pl.ds(pl.multiple_of((1 - at_ref[4]) * w + tile, TILE), TILE)
        out_ref[:, mine] = base_ref[:, mine] + 0.25 * total
        out_ref[:, other] = base_ref[:, other]


def early_sums(prior, xt, runs):
    operands, spans = listed(runs)
    rows, cols = prior.shape
    return pl.pallas_call(
        functools.partial(early_kernel, spans),
        in_specs=[VMEM] * (2 + len(operands)),
        out_specs=[VMEM] * 2,
        out_shape=[
            jax.ShapeDtypeStruct((2, 2 * rows, cols // 2), jnp.float32),
            jax.ShapeDtypeStruct(prior.shape, jnp.float32),
        ],
        compiler_params=pltpu.CompilerParams(vmem_limit_bytes=8 * 2**20),
        cost_estimate=pl.CostEstimate(flops=3 * rows * xt.shape[2] * cols, bytes_accessed=0, transcendentals=0),
    )(prior, xt, *operands)


def late_call(kernel, first, specs, sums, xt, runs, shape):
    operands, spans = listed(runs)
    return pl.pallas_call(
        functools.partial(kernel, spans),
        in_specs=specs + [VMEM] * (2 + len(operands)),
        out_specs=VMEM,
        out_shape=jax.ShapeDtypeStruct(shape, jnp.float32),
        compiler_params=pltpu.CompilerParams(vmem_limit_bytes=8 * 2**20),
        cost_estimate=pl.CostEstimate(flops=sums.size * 500, bytes_accessed=0, transcendentals=0),
    )(*first, sums, xt, *operands)


def late_theirs(sums, xt, runs):
    return late_call(theirs_kernel, (), [], sums, xt, runs, (sums.shape[1] // 2, sums.shape[2]))


def late_mine(at, base, sums, xt, runs):
    return late_call(mine_kernel, (at, base), [pl.BlockSpec(memory_space=pltpu.SMEM), VMEM], sums, xt, runs, base.shape)


def both(array, *index):
    return [(array, index + (0,)), (array, index + (1,))]


def in_order(first, mine, other, axis):
    return jnp.concatenate([jnp.where(first, mine, other), jnp.where(first, other, mine)], axis)


def on_device(saved_inputs, output_grads, fisher_prior):
    first = lax.axis_index("c") == 0
    at = jnp.stack([lax.axis_index(name) for name in ("zh", "x", "zl", "y", "c")]).astype(jnp.int32)
    seqs, toks, cols = output_grads.shape
    half = cols // 2
    token = jnp.zeros((8, 128), jnp.float32)

    left, right = output_grads[..., :half], output_grads[..., half:]
    got = fetch(jnp.where(first, right, left), c=1)
    unit = jnp.concatenate([jnp.where(first, left, right), got], axis=1)

    unit0, unit1 = unit[0], unit[1]
    (unit, unit0, unit1), token = stage(token, (unit, unit0, unit1))
    above0, below0 = fetch(unit0, zh=1), fetch(unit0, zh=-1)
    ahead, behind = fetch(unit, x=1), fetch(unit, x=-1)
    turn1 = fetch(saved_inputs, y=1)

    (above0, below0, turn1, unit1), token = stage(token, (above0, below0, turn1, unit1), (ahead, behind))
    above1, below1 = fetch(unit1, zh=1), fetch(unit1, zh=-1)
    first_ahead = fetch(jnp.stack([ahead[1], above0, below0]), x=1)
    first_behind = fetch(jnp.stack([behind[0], above0, below0]), x=-1)
    turn2 = fetch(turn1, y=1)

    (above1, below1, below0, turn2), token = stage(token, (above1, below1, below0, turn2))
    opp0, opp1 = fetch(below0, zh=-1), fetch(above1, zh=1)

    sides = jnp.stack([above1, below1])
    (sides, turn2), token = stage(token, (sides, turn2), (first_ahead, first_behind))
    second_ahead, second_behind = fetch(sides, x=1), fetch(sides, x=-1)
    turn3 = fetch(turn2, y=1)
    turns = jnp.stack([saved_inputs, turn1, turn2, turn3])

    (opp0, opp1, turns), token = stage(token, (opp0, opp1, turns))
    opp = jnp.stack([opp0, opp1])
    opp_ahead, opp_behind = fetch(opp, x=1), fetch(opp, x=-1)
    met = fetch(turns, zl=1)

    (second_ahead, second_behind), token = stage(token, (second_ahead, second_behind))
    above_far = fetch(jnp.stack([first_behind[1], second_behind[0]]), x=-1)
    below_far = fetch(jnp.stack([first_ahead[2], second_ahead[1]]), x=1)

    (opp_ahead, opp_behind, turns), token = stage(token, (opp_ahead, opp_behind, turns))
    opp_far0, opp_far1 = fetch(opp_behind[0], x=-1), fetch(opp_ahead[1], x=1)
    sib, sib_met = fetch(turns, c=1), fetch(met, c=1)
    xt = turned(at, turns, met, sib, sib_met)

    early = [both(unit), both(ahead), [(first_behind, (0,)), (first_ahead, (0,))], both(behind)]
    early.append([(above0, ()), (above1, ())])
    early.append([(first_ahead, (1,)), (second_ahead, (0,))])
    early.append([(first_behind, (1,)), (second_behind, (0,))])
    early.append([(below0, ()), (below1, ())])
    early.append([(first_ahead, (2,)), (second_ahead, (1,))])
    early.append([(first_behind, (2,)), (second_behind, (1,))])
    early += [both(opp), both(opp_ahead)]
    late = [both(opp_behind), both(above_far), [(opp_far0, ()), (opp_far1, ())], both(below_far)]
    sums, base = early_sums(fisher_prior, xt, [(0, early)])
    runs = [(len(early) * 2 * toks, late)]
    back = 0.25 * fetch(late_theirs(sums, xt, runs), c=1)
    out = late_mine(at, base, sums, xt, runs)
    return out + in_order(first, jnp.zeros_like(back), back, 1)


def solution(mesh):
    fine = Mesh(mesh.devices.reshape(tuple(SIZES.values())), AXES)
    inp, out = ("zh", "x", "c"), ("zl", "y")
    return jax.shard_map(
        on_device,
        mesh=fine,
        in_specs=(P(None, out, inp), P(None, inp, out), P(inp, out)),
        out_specs=P(inp, out),
        check_vma=False,
    )
```
